32 devices in a mesh: cells: 16 (over z, x, core), species: 2 (over y).
Axes of the slice: x: 2, y: 2, z: 4, core: 2. Of those that a mesh axis runs over, the one named last changes fastest.
Arguments:
- covariates: bfloat16 [64, 256, 1024], P(None, 'cells'), may hold values from -6 to 6
- coefficients: bfloat16 [64, 8192], P('cells', 'species'), may hold values from -0.75 to 0.75
- intercept: float32 [8192], P('species'), may hold values from -6 to 6
- traits: bfloat16 [8192, 32], P('species'), may hold values from -6 to 6
- land_weight: int32 [256, 1024], P('cells'), may hold values from 0 to 3
Outputs:
- smoothed: float32 [32, 256, 1024], P('species', 'cells')
The draws below stay inside these ranges and needn't reach their ends.
All inputs are finite; a program needn't handle non-finite values.
Results may differ from the reference program's by a relative error of at most 0.0015.
Values may be sent and summed in bfloat16 or wider, within the bound.
A program may use at most 64 MiB of HBM per device.

```python
import jax
import jax.numpy as jnp
from jax import lax

SPECIES = 8192
NCOV = 64
TRAITS = 32
COLS = 1024
SWEEPS = 8
NROWS = 256


def plant(result, rng, smallest, high):
    longest = result.shape.index(max(result.shape))
    spots = []
    for shift in (0, 1):
        where = [jax.random.randint(jax.random.fold_in(rng, axis), (), 0, length) for axis, length in enumerate(result.shape)]
        where[longest] = (where[longest] + shift) % result.shape[longest]
        spots.append(tuple(where))
    return result.at[spots[0]].set(smallest).at[spots[1]].set(high)


def strengthened(entries, own_key, source, target, parts, factor):
    def block_of(dim):
        return (jnp.arange(entries.shape[dim]) // (entries.shape[dim] // parts)).reshape((-1,) + (1,) * (entries.ndim - 1 - dim))

    first = jax.random.permutation(own_key, parts)[block_of(target)]
    second = (block_of(target) + parts // 2) % parts
    return jnp.where((block_of(source) == first) | (block_of(source) == second), factor * entries, entries)


def block_levels(own_key, extent, cuts, low, largest):
    def one(position, parts):
        steps = jax.random.uniform(jax.random.fold_in(jax.random.fold_in(own_key, 6), position), (parts,), jnp.float32, low / len(cuts), largest / len(cuts))
        return jnp.repeat(jnp.exp(steps), extent[position] // parts).reshape((-1,) + (1,) * (len(extent) - position - 1))

    loudness = one(*cuts[0])
    for cut in cuts[1:]:
        loudness = loudness * one(*cut)
    return loudness


def gaussian(rng, shape, width, most, pieces=(), held_as=jnp.bfloat16):
    factor_of = block_levels(rng, shape, pieces, -0.22, 0.18) if pieces else 1.0
    values = jax.random.normal(rng, shape, jnp.float32) * width * factor_of
    return jnp.minimum(jnp.maximum(values, -most), most).astype(held_as)


def heavy_noise(key, extent, spread, limit, shards, heavy, kind=jnp.bfloat16):
    entries = spread * jax.random.normal(key, extent, jnp.float32)
    if shards:
        entries = entries * block_levels(key, extent, shards, -0.22, 0.18)
    return jnp.clip(strengthened(entries, jax.random.fold_in(key, 3), *heavy), -limit, limit).astype(kind)


def setup_inputs(seed: int = 0) -> dict:
    splits = jax.random.split(jax.random.key(seed), 6)
    covariates = gaussian(splits[0], (NCOV, NROWS, COLS), 1.0, 6.0, ((1, 16),))
    coefficients = gaussian(splits[1], (NCOV, SPECIES), NCOV ** -0.5, 0.75, ((0, 16), (1, 2)))
    intercept = gaussian(splits[2], (SPECIES,), 1.5, 6.0, ((0, 2),), jnp.float32)
    traits = heavy_noise(splits[3], (SPECIES, TRAITS), 1.0, 6.0, ((0, 2),), (0, 1, 2, 2.0))
    land_weight = plant(jax.random.randint(splits[4], (NROWS, COLS), 0, 4), jax.random.fold_in(splits[4], 1), 0, 3).astype(jnp.int32)
    return dict(covariates=covariates, coefficients=coefficients, intercept=intercept, traits=traits, land_weight=land_weight)


coupling = 1.0


def neighbours(values):
    padded = jnp.pad(values, ((0, 0), (1, 1), (1, 1)))
    return padded[:, 2:, 1:-1] + padded[:, :-2, 1:-1] + padded[:, 1:-1, 2:] + padded[:, 1:-1, :-2]


def reference(covariates, coefficients, intercept, traits, land_weight):
    cell_count = NROWS * COLS
    block_len = min(2048, cell_count)
    block_count = cell_count // block_len
    blocks = covariates.reshape(NCOV, block_count, block_len).transpose(1, 0, 2)
    species_rows = coefficients.T
    trait_rows = traits.T

    def block_maps(columns):
        logits_block = jnp.dot(species_rows, columns, preferred_element_type=jnp.float32) + intercept[:, None]
        presence = jax.nn.sigmoid(logits_block).astype(jnp.bfloat16)
        numerator = jnp.dot(trait_rows, presence, preferred_element_type=jnp.float32)
        cover = jnp.sum(presence.astype(jnp.float32), axis=0)
        return numerator / cover[None, :]

    mean_traits = lax.map(block_maps, blocks)
    mean_traits = mean_traits.transpose(1, 0, 2).reshape(TRAITS, NROWS, COLS)
    land_float = land_weight.astype(jnp.float32)[None]
    divisor = 1.0 + coupling * land_float * neighbours(land_float)
    smoothed = mean_traits
    for sweep in range(SWEEPS):
        smoothed = (mean_traits + coupling * land_float * neighbours(land_float * smoothed)) / divisor
    return smoothed
```

```python
import functools

import jax
import jax.numpy as jnp
from jax import lax
from jax.experimental import pallas as pl
from jax.experimental.pallas import tpu as pltpu
from jax.sharding import PartitionSpec as P

SWEEPS = 8
F32 = jnp.float32
BF16 = jnp.bfloat16


def sums_kernel(per, rows_per_group, cov_ref, w_ref, trait_ref, *out_refs):
    blocks, trait_rows, block_len = trait_ref.shape
    cells = cov_ref[...]

    def total(presence_of):
        acc = jnp.zeros((trait_rows, cells.shape[1]), F32)
        for j in range(blocks):
            half = jnp.dot(
                w_ref[j * block_len : (j + 1) * block_len, :], cells, preferred_element_type=F32
            )
            presence = presence_of(half).astype(BF16)
            acc = acc + jnp.dot(trait_ref[j], presence, preferred_element_type=F32)
        return acc

    def put(acc):
        for g, out_ref in enumerate(out_refs):
            out_ref[0] = acc[g * rows_per_group : (g + 1) * rows_per_group]

    acc = total(lambda half: 0.5 * jnp.tanh(half) + 0.5)
    put(acc)
    rare = jnp.min(acc[per : per + 1, :]) < blocks * block_len / 64.0

    @pl.when(rare)
    def _():
        put(total(lambda half: 1.0 / (1.0 + jnp.exp(-2.0 * half))))


def species_sums(cov_ext, w, trait_blocks, first, count, cols, per, groups, rows_per_group):
    depth = cov_ext.shape[0]
    species = w.shape[0]
    out = jax.ShapeDtypeStruct((count, rows_per_group, cols), F32)
    return pl.pallas_call(
        functools.partial(sums_kernel, per, rows_per_group),
        grid=(count,),
        in_specs=[
            pl.BlockSpec((depth, cols), lambda i: (0, i + first)),
            pl.BlockSpec(w.shape, lambda i: (0, 0)),
            pl.BlockSpec(trait_blocks.shape, lambda i: (0, 0, 0)),
        ],
        out_specs=[pl.BlockSpec((1, rows_per_group, cols), lambda i: (i, 0, 0))] * groups,
        out_shape=[out] * groups,
        compiler_params=pltpu.CompilerParams(vmem_limit_bytes=40 << 20),
        cost_estimate=pl.CostEstimate(
            flops=2 * species * 512 * cols * count,
            bytes_accessed=4 * groups * rows_per_group * cols * count,
            transcendentals=species * cols * count,
        ),
    )(cov_ext, w, trait_blocks)


def smooth_kernel(starts, land_ref, gain_ref, inverse_ref, *refs):
    mean_refs = refs[: len(starts)]
    out_ref, base, even, odd = refs[len(starts) :]
    ext, per, cols = base.shape
    column = lax.broadcasted_iota(jnp.int32, (1, cols), 1)
    not_first = (column > 0).astype(F32)
    not_last = (column < cols - 1).astype(F32)

    def around(held, r):
        here = held[r]
        sides = pltpu.roll(here, 1, 1) * not_first + pltpu.roll(here, cols - 1, 1) * not_last
        return (held[r - 1] + held[r + 1]) + sides

    for start, mean_ref in zip(starts, mean_refs):

        @pl.loop(0, mean_ref.shape[0])
        def _(i):
            r = start + i
            scaled = mean_ref[i] * land_ref[r]
            even[r] = scaled
            base[r] = scaled * inverse_ref[r]

    for sweep in range(1, SWEEPS):
        source, target = (even, odd) if sweep % 2 else (odd, even)

        @pl.loop(sweep, ext - sweep, unroll=2)
        def _(r):
            target[r] = base[r] + gain_ref[r] * around(source, r)

    source = odd if SWEEPS % 2 == 0 else even
    for start, mean_ref in zip(starts, mean_refs):
        if SWEEPS <= start < ext - SWEEPS:

            @pl.loop(0, mean_ref.shape[0], unroll=2)
            def _(i):
                r = start + i
                out_ref[r - SWEEPS] = (
                    mean_ref[i] + land_ref[r] * around(source, r)
                ) * inverse_ref[r]


def local(covariates, coefficients, intercept, traits, land_weight):
    ncov, rows, cols = covariates.shape
    species, trait_count = traits.shape
    groups = lax.axis_size("species")
    count = lax.axis_size("cells")
    per = trait_count // groups
    rows_per_group = -(-(per + 1) // 8) * 8
    ahead = [(i, i + 1) for i in range(count - 1)]
    back = [(target, source) for source, target in ahead]

    gathered = lax.all_gather(coefficients, "cells", axis=0, tiled=True)
    rounded = functools.partial(lax.reduce_precision, exponent_bits=8, mantissa_bits=7)
    bias = 0.5 * intercept
    high = rounded(bias)
    middle = rounded(bias - high)
    low = bias - high - middle
    spare = 13
    w = jnp.concatenate(
        [
            gathered * jnp.asarray(0.5, BF16),
            jnp.stack([high, middle, low]).astype(BF16),
            jnp.zeros((spare, species), BF16),
        ]
    ).T
    cov_ext = jnp.concatenate(
        [
            covariates.reshape(ncov, rows * cols),
            jnp.ones((3, rows * cols), BF16),
            jnp.zeros((spare, rows * cols), BF16),
        ]
    )
    grouped = jnp.roll(traits.T.reshape(groups, per, species), -lax.axis_index("species"), axis=0)
    grouped = jnp.concatenate(
        [
            grouped,
            jnp.ones((groups, 1, species), BF16),
            jnp.zeros((groups, rows_per_group - per - 1, species), BF16),
        ],
        axis=1,
    )
    block_len = min(512, species)
    trait_blocks = grouped.reshape(
        groups * rows_per_group, species // block_len, block_len
    ).transpose(1, 0, 2)

    below = lax.ppermute(land_weight[-SWEEPS:], "cells", ahead)
    above = lax.ppermute(land_weight[:SWEEPS], "cells", back)
    land = jnp.concatenate([below, land_weight, above]).astype(F32)
    padded = jnp.pad(land, 1)
    inverse = 1.0 / (
        1.0
        + land * (padded[2:, 1:-1] + padded[:-2, 1:-1] + padded[1:-1, 2:] + padded[1:-1, :-2])
    )
    gain = land * land * inverse

    quarter = SWEEPS // 2
    order = [0] + [rows - quarter] + list(range(quarter, rows - quarter, quarter))
    own, halo = {}, {}
    for first in order:
        sums = species_sums(
            cov_ext, w, trait_blocks, first, quarter, cols, per, groups, rows_per_group
        )
        whole = sums[0]
        for shift in range(1, groups):
            perm = [(i, (i + shift) % groups) for i in range(groups)]
            whole = whole + lax.ppermute(sums[shift], "species", perm)
        mean = whole[:, :per] / whole[:, per : per + 1]
        own[SWEEPS + first] = mean
        if first < SWEEPS:
            halo[SWEEPS + rows + first] = lax.ppermute(mean, "cells", back)
        if first >= rows - SWEEPS:
            halo[first - (rows - SWEEPS)] = lax.ppermute(mean, "cells", ahead)
    parts = {**own, **halo}
    starts = sorted(parts)
    ext = rows + 2 * SWEEPS
    smoothed = pl.pallas_call(
        functools.partial(smooth_kernel, starts),
        out_shape=jax.ShapeDtypeStruct((rows, per, cols), F32),
        scratch_shapes=[pltpu.VMEM((ext, per, cols), F32)] * 3,
        compiler_params=pltpu.CompilerParams(vmem_limit_bytes=40 << 20),
    )(land[:, None], gain[:, None], inverse[:, None], *[parts[s] for s in starts])
    return smoothed.transpose(1, 0, 2)


def solution(mesh):
    return jax.shard_map(
        local,
        mesh=mesh,
        in_specs=(
            P(None, "cells", None),
            P("cells", "species"),
            P("species"),
            P("species", None),
            P("cells", None),
        ),
        out_specs=P("species", "cells", None),
        check_vma=False,
    )
```

```python
import functools

import jax
import jax.numpy as jnp
from jax import lax
from jax.experimental import pallas as pl
from jax.experimental.pallas import tpu as pltpu
from jax.sharding import PartitionSpec as P

SWEEPS = 8
F32 = jnp.float32
BF16 = jnp.bfloat16


def sums_kernel(per, rows_per_group, cov_ref, w_ref, trait_ref, *out_refs):
    blocks, trait_rows, block_len = trait_ref.shape
    cells = cov_ref[...]

    def total(presence_of):
        acc = jnp.zeros((trait_rows, cells.shape[1]), F32)
        for j in range(blocks):
            half = jnp.dot(
                w_ref[j * block_len : (j + 1) * block_len, :], cells, preferred_element_type=F32
            )
            presence = presence_of(half).astype(BF16)
            acc = acc + jnp.dot(trait_ref[j], presence, preferred_element_type=F32)
        return acc

    def put(acc):
        for g, out_ref in enumerate(out_refs):
            out_ref[0] = acc[g * rows_per_group : (g + 1) * rows_per_group]

    acc = total(lambda half: 0.5 * jnp.tanh(half) + 0.5)
    put(acc)
    rare = jnp.min(acc[per : per + 1, :]) < blocks * block_len / 64.0

    @pl.when(rare)
    def _():
        put(total(lambda half: 1.0 / (1.0 + jnp.exp(-2.0 * half))))


def species_sums(cov_ext, w, trait_blocks, first, count, cols, per, groups, rows_per_group):
    depth = cov_ext.shape[0]
    species = w.shape[0]
    out = jax.ShapeDtypeStruct((count, rows_per_group, cols), F32)
    return pl.pallas_call(
        functools.partial(sums_kernel, per, rows_per_group),
        grid=(count,),
        in_specs=[
            pl.BlockSpec((depth, cols), lambda i: (0, i + first)),
            pl.BlockSpec(w.shape, lambda i: (0, 0)),
            pl.BlockSpec(trait_blocks.shape, lambda i: (0, 0, 0)),
        ],
        out_specs=[pl.BlockSpec((1, rows_per_group, cols), lambda i: (i, 0, 0))] * groups,
        out_shape=[out] * groups,
        compiler_params=pltpu.CompilerParams(vmem_limit_bytes=40 << 20),
        cost_estimate=pl.CostEstimate(
            flops=2 * species * 512 * cols * count,
            bytes_accessed=4 * groups * rows_per_group * cols * count,
            transcendentals=species * cols * count,
        ),
    )(cov_ext, w, trait_blocks)


def smooth_kernel(starts, land_ref, gain_ref, inverse_ref, *refs):
    mean_refs = refs[: len(starts)]
    out_ref, base, even, odd = refs[len(starts) :]
    ext, per, cols = base.shape
    column = lax.broadcasted_iota(jnp.int32, (1, cols), 1)
    not_first = (column > 0).astype(F32)
    not_last = (column < cols - 1).astype(F32)

    def around(held, r):
        here = held[r]
        sides = pltpu.roll(here, 1, 1) * not_first + pltpu.roll(here, cols - 1, 1) * not_last
        return (held[r - 1] + held[r + 1]) + sides

    for start, mean_ref in zip(starts, mean_refs):

        @pl.loop(0, mean_ref.shape[0])
        def _(i):
            r = start + i
            scaled = mean_ref[i] * land_ref[r]
            even[r] = scaled
            base[r] = scaled * inverse_ref[r]

    for sweep in range(1, SWEEPS):
        source, target = (even, odd) if sweep % 2 else (odd, even)

        @pl.loop(sweep, ext - sweep, unroll=4 if (ext - 2 * sweep) % 4 == 0 else 2)
        def _(r):
            target[r] = base[r] + gain_ref[r] * around(source, r)

    source = odd if SWEEPS % 2 == 0 else even
    for start, mean_ref in zip(starts, mean_refs):
        if SWEEPS <= start < ext - SWEEPS:

            @pl.loop(0, mean_ref.shape[0])
            def _(i):
                r = start + i
                out_ref[r - SWEEPS] = (
                    mean_ref[i] + land_ref[r] * around(source, r)
                ) * inverse_ref[r]


def gather_kernel(count, block_ref, out_ref, send_sem, recv_sem):
    me = lax.axis_index("cells")
    peers = [lax.rem(me + shift, count) for shift in range(1, count)]
    barrier = pltpu.get_barrier_semaphore()
    for peer in peers:
        pl.semaphore_signal(
            barrier, inc=1, device_id={"cells": peer}, device_id_type=pl.DeviceIdType.MESH
        )
    pl.semaphore_wait(barrier, count - 1)
    copies = [
        pltpu.make_async_remote_copy(
            src_ref=block_ref,
            dst_ref=out_ref.at[me],
            send_sem=send_sem.at[slot],
            recv_sem=recv_sem.at[slot],
            device_id={"cells": peer},
            device_id_type=pl.DeviceIdType.MESH,
        )
        for slot, peer in enumerate(peers)
    ]
    for copy in copies:
        copy.start()
    out_ref[me] = block_ref[...]
    for copy in copies:
        copy.wait()


def gather(coefficients, count):
    own, species = coefficients.shape
    tile = 16
    folds = max(1, tile // own)
    while (species // folds) % 128:
        folds //= 2
    width = species // folds
    block = coefficients.reshape(own, folds, width).transpose(1, 0, 2).reshape(own * folds, width)
    filled = -(-own * folds // tile) * tile
    block = jnp.pad(block, ((0, filled - own * folds), (0, 0)))
    blocks = pl.pallas_call(
        functools.partial(gather_kernel, count),
        out_shape=jax.ShapeDtypeStruct((count, filled, width), BF16),
        in_specs=[pl.BlockSpec(memory_space=pltpu.VMEM)],
        out_specs=pl.BlockSpec(memory_space=pltpu.VMEM),
        scratch_shapes=[pltpu.SemaphoreType.DMA((count - 1,))] * 2,
        compiler_params=pltpu.CompilerParams(collective_id=0, has_side_effects=True),
    )(block)
    blocks = blocks[:, : own * folds].reshape(count, folds, own, width)
    return blocks.transpose(0, 2, 1, 3).reshape(count * own, species)


def local(covariates, coefficients, intercept, traits, land_weight):
    ncov, rows, cols = covariates.shape
    species, trait_count = traits.shape
    groups = lax.axis_size("species")
    count = lax.axis_size("cells")
    per = trait_count // groups
    rows_per_group = -(-(per + 1) // 8) * 8
    ahead = [(i, i + 1) for i in range(count - 1)]
    back = [(target, source) for source, target in ahead]

    gathered = gather(coefficients, count)
    rounded = functools.partial(lax.reduce_precision, exponent_bits=8, mantissa_bits=7)
    bias = 0.5 * intercept
    high = rounded(bias)
    middle = rounded(bias - high)
    low = bias - high - middle
    spare = 13
    w = jnp.concatenate(
        [
            gathered * jnp.asarray(0.5, BF16),
            jnp.stack([high, middle, low]).astype(BF16),
            jnp.zeros((spare, species), BF16),
        ]
    ).T
    cov_ext = jnp.concatenate(
        [
            covariates.reshape(ncov, rows * cols),
            jnp.ones((3, rows * cols), BF16),
            jnp.zeros((spare, rows * cols), BF16),
        ]
    )
    grouped = jnp.roll(traits.T.reshape(groups, per, species), -lax.axis_index("species"), axis=0)
    grouped = jnp.concatenate(
        [
            grouped,
            jnp.ones((groups, 1, species), BF16),
            jnp.zeros((groups, rows_per_group - per - 1, species), BF16),
        ],
        axis=1,
    )
    block_len = min(512, species)
    trait_blocks = grouped.reshape(
        groups * rows_per_group, species // block_len, block_len
    ).transpose(1, 0, 2)

    below = lax.ppermute(land_weight[-SWEEPS:], "cells", ahead)
    above = lax.ppermute(land_weight[:SWEEPS], "cells", back)
    land = jnp.concatenate([below, land_weight, above]).astype(F32)
    padded = jnp.pad(land, 1)
    inverse = 1.0 / (
        1.0
        + land * (padded[2:, 1:-1] + padded[:-2, 1:-1] + padded[1:-1, 2:] + padded[1:-1, :-2])
    )
    gain = land * land * inverse

    last = 3 if rows - SWEEPS > 3 else 0
    chunks = [(0, SWEEPS), (SWEEPS, rows - SWEEPS - last), (rows - last, last)]
    own, halo = {}, {}
    for first, size in [c for c in chunks if c[1]]:
        sums = species_sums(
            cov_ext, w, trait_blocks, first, size, cols, per, groups, rows_per_group
        )
        whole = sums[0]
        for shift in range(1, groups):
            perm = [(i, (i + shift) % groups) for i in range(groups)]
            whole = whole + lax.ppermute(sums[shift], "species", perm)
        mean = whole[:, :per] / whole[:, per : per + 1]
        own[SWEEPS + first] = mean
        if first < SWEEPS:
            halo[SWEEPS + rows + first] = lax.ppermute(mean, "cells", back)
        if first >= rows - SWEEPS:
            halo[first - (rows - SWEEPS)] = lax.ppermute(mean, "cells", ahead)
    parts = {**own, **halo}
    starts = sorted(parts)
    ext = rows + 2 * SWEEPS
    smoothed = pl.pallas_call(
        functools.partial(smooth_kernel, starts),
        out_shape=jax.ShapeDtypeStruct((rows, per, cols), F32),
        scratch_shapes=[pltpu.VMEM((ext, per, cols), F32)] * 3,
        compiler_params=pltpu.CompilerParams(vmem_limit_bytes=40 << 20),
    )(land[:, None], gain[:, None], inverse[:, None], *[parts[s] for s in starts])
    return smoothed.transpose(1, 0, 2)


def solution(mesh):
    return jax.shard_map(
        local,
        mesh=mesh,
        in_specs=(
            P(None, "cells", None),
            P("cells", "species"),
            P("species"),
            P("species", None),
            P("cells", None),
        ),
        out_specs=P("species", "cells", None),
        check_vma=False,
    )
```

```python
import functools

import jax
import jax.numpy as jnp
from jax import lax
from jax.experimental import pallas as pl
from jax.experimental.pallas import tpu as pltpu
from jax.sharding import PartitionSpec as P

SWEEPS = 8
F32 = jnp.float32
BF16 = jnp.bfloat16


def sums_kernel(per, rows_per_group, cov_ref, w_ref, trait_ref, *out_refs):
    blocks, trait_rows, block_len = trait_ref.shape
    cells = cov_ref[...]

    def total(presence_of):
        acc = jnp.zeros((trait_rows, cells.shape[1]), F32)
        for j in range(blocks):
            half = jnp.dot(
                w_ref[j * block_len : (j + 1) * block_len, :], cells, preferred_element_type=F32
            )
            presence = presence_of(half).astype(BF16)
            acc = acc + jnp.dot(trait_ref[j], presence, preferred_element_type=F32)
        return acc

    def put(acc):
        for g, out_ref in enumerate(out_refs):
            out_ref[0] = acc[g * rows_per_group : (g + 1) * rows_per_group]

    acc = total(lambda half: 0.5 * jnp.tanh(half) + 0.5)
    put(acc)
    rare = jnp.min(acc[per : per + 1, :]) < blocks * block_len / 64.0

    @pl.when(rare)
    def _():
        put(total(lambda half: 1.0 / (1.0 + jnp.exp(-2.0 * half))))


def species_sums(cov_ext, w, trait_blocks, first, count, cols, per, groups, rows_per_group):
    depth = cov_ext.shape[0]
    species = w.shape[0]
    out = jax.ShapeDtypeStruct((count, rows_per_group, cols), F32)
    return pl.pallas_call(
        functools.partial(sums_kernel, per, rows_per_group),
        grid=(count,),
        in_specs=[
            pl.BlockSpec((depth, cols), lambda i: (0, i + first)),
            pl.BlockSpec(w.shape, lambda i: (0, 0)),
            pl.BlockSpec(trait_blocks.shape, lambda i: (0, 0, 0)),
        ],
        out_specs=[pl.BlockSpec((1, rows_per_group, cols), lambda i: (i, 0, 0))] * groups,
        out_shape=[out] * groups,
        compiler_params=pltpu.CompilerParams(vmem_limit_bytes=40 << 20),
        cost_estimate=pl.CostEstimate(
            flops=2 * species * 512 * cols * count,
            bytes_accessed=4 * groups * rows_per_group * cols * count,
            transcendentals=species * cols * count,
        ),
    )(cov_ext, w, trait_blocks)


def smooth_kernel(starts, land_ref, gain_ref, inverse_ref, *refs):
    mean_refs = refs[: len(starts)]
    out_ref, base, even, odd = refs[len(starts) :]
    ext, per, cols = base.shape
    column = lax.broadcasted_iota(jnp.int32, (1, cols), 1)
    not_first = (column > 0).astype(F32)
    not_last = (column < cols - 1).astype(F32)

    def around(held, r):
        here = held[r]
        sides = pltpu.roll(here, 1, 1) * not_first + pltpu.roll(here, cols - 1, 1) * not_last
        return (held[r - 1] + held[r + 1]) + sides

    for start, mean_ref in zip(starts, mean_refs):

        @pl.loop(0, mean_ref.shape[0])
        def _(i):
            r = start + i
            scaled = mean_ref[i] * land_ref[r]
            even[r] = scaled
            base[r] = scaled * inverse_ref[r]

    for sweep in range(1, SWEEPS):
        source, target = (even, odd) if sweep % 2 else (odd, even)

        @pl.loop(sweep, ext - sweep, unroll=4 if (ext - 2 * sweep) % 4 == 0 else 2)
        def _(r):
            target[r] = base[r] + gain_ref[r] * around(source, r)

    source = odd if SWEEPS % 2 == 0 else even
    for start, mean_ref in zip(starts, mean_refs):
        if SWEEPS <= start < ext - SWEEPS:

            @pl.loop(0, mean_ref.shape[0])
            def _(i):
                r = start + i
                out_ref[r - SWEEPS] = (
                    mean_ref[i] + land_ref[r] * around(source, r)
                ) * inverse_ref[r]


def gather_kernel(count, block_ref, out_ref, send_sem, recv_sem):
    me = lax.axis_index("cells")
    peers = [lax.rem(me + shift, count) for shift in range(1, count)]
    barrier = pltpu.get_barrier_semaphore()
    for peer in peers:
        pl.semaphore_signal(
            barrier, inc=1, device_id={"cells": peer}, device_id_type=pl.DeviceIdType.MESH
        )
    pl.semaphore_wait(barrier, count - 1)
    copies = [
        pltpu.make_async_remote_copy(
            src_ref=block_ref,
            dst_ref=out_ref.at[me],
            send_sem=send_sem.at[slot],
            recv_sem=recv_sem.at[slot],
            device_id={"cells": peer},
            device_id_type=pl.DeviceIdType.MESH,
        )
        for slot, peer in enumerate(peers)
    ]
    for copy in copies:
        copy.start()
    out_ref[me] = block_ref[...]
    for copy in copies:
        copy.wait()


def gather(coefficients, count):
    own, species = coefficients.shape
    tile = 16
    folds = max(1, tile // own)
    while (species // folds) % 128:
        folds //= 2
    width = species // folds
    block = coefficients.reshape(own, folds, width).transpose(1, 0, 2).reshape(own * folds, width)
    filled = -(-own * folds // tile) * tile
    block = jnp.pad(block, ((0, filled - own * folds), (0, 0)))
    blocks = pl.pallas_call(
        functools.partial(gather_kernel, count),
        out_shape=jax.ShapeDtypeStruct((count, filled, width), BF16),
        in_specs=[pl.BlockSpec(memory_space=pltpu.VMEM)],
        out_specs=pl.BlockSpec(memory_space=pltpu.VMEM),
        scratch_shapes=[pltpu.SemaphoreType.DMA((count - 1,))] * 2,
        compiler_params=pltpu.CompilerParams(collective_id=0, has_side_effects=True),
    )(block)
    blocks = blocks[:, : own * folds].reshape(count, folds, own, width)
    return blocks.transpose(0, 2, 1, 3).reshape(count * own, species)


def local(covariates, coefficients, intercept, traits, land_weight):
    ncov, rows, cols = covariates.shape
    species, trait_count = traits.shape
    groups = lax.axis_size("species")
    count = lax.axis_size("cells")
    per = trait_count // groups
    rows_per_group = -(-(per + 1) // 8) * 8
    ahead = [(i, i + 1) for i in range(count - 1)]
    back = [(target, source) for source, target in ahead]

    gathered = gather(coefficients, count)
    rounded = functools.partial(lax.reduce_precision, exponent_bits=8, mantissa_bits=7)
    bias = 0.5 * intercept
    high = rounded(bias)
    middle = rounded(bias - high)
    low = bias - high - middle
    spare = 13
    w = jnp.concatenate(
        [
            gathered * jnp.asarray(0.5, BF16),
            jnp.stack([high, middle, low]).astype(BF16),
            jnp.zeros((spare, species), BF16),
        ]
    ).T
    cov_ext = jnp.concatenate(
        [
            covariates.reshape(ncov, rows * cols),
            jnp.ones((3, rows * cols), BF16),
            jnp.zeros((spare, rows * cols), BF16),
        ]
    )
    grouped = jnp.roll(traits.T.reshape(groups, per, species), -lax.axis_index("species"), axis=0)
    grouped = jnp.concatenate(
        [
            grouped,
            jnp.ones((groups, 1, species), BF16),
            jnp.zeros((groups, rows_per_group - per - 1, species), BF16),
        ],
        axis=1,
    )
    block_len = min(512, species)
    trait_blocks = grouped.reshape(
        groups * rows_per_group, species // block_len, block_len
    ).transpose(1, 0, 2)

    below = lax.ppermute(land_weight[-SWEEPS:], "cells", ahead)
    above = lax.ppermute(land_weight[:SWEEPS], "cells", back)
    land = jnp.concatenate([below, land_weight, above]).astype(F32)
    padded = jnp.pad(land, 1)
    inverse = 1.0 / (
        1.0
        + land * (padded[2:, 1:-1] + padded[:-2, 1:-1] + padded[1:-1, 2:] + padded[1:-1, :-2])
    )
    gain = land * land * inverse

    last = 3 if rows - SWEEPS > 3 else 0
    chunks = [(0, SWEEPS), (SWEEPS, rows - SWEEPS - last), (rows - last, last)]
    own, halo = {}, {}
    for first, size in [c for c in chunks if c[1]]:
        if first > SWEEPS:
            trait_blocks, own[SWEEPS] = lax.optimization_barrier((trait_blocks, own[SWEEPS]))
            halo[SWEEPS + rows] = lax.ppermute(own[SWEEPS], "cells", back)
        sums = species_sums(
            cov_ext, w, trait_blocks, first, size, cols, per, groups, rows_per_group
        )
        whole = sums[0]
        for shift in range(1, groups):
            perm = [(i, (i + shift) % groups) for i in range(groups)]
            whole = whole + lax.ppermute(sums[shift], "species", perm)
        mean = whole[:, :per] / whole[:, per : per + 1]
        own[SWEEPS + first] = mean
        if first < SWEEPS and not last:
            halo[SWEEPS + rows + first] = lax.ppermute(mean, "cells", back)
        if first >= rows - SWEEPS:
            halo[first - (rows - SWEEPS)] = lax.ppermute(mean, "cells", ahead)
    parts = {**own, **halo}
    starts = sorted(parts)
    ext = rows + 2 * SWEEPS
    smoothed = pl.pallas_call(
        functools.partial(smooth_kernel, starts),
        out_shape=jax.ShapeDtypeStruct((rows, per, cols), F32),
        scratch_shapes=[pltpu.VMEM((ext, per, cols), F32)] * 3,
        compiler_params=pltpu.CompilerParams(vmem_limit_bytes=40 << 20),
    )(land[:, None], gain[:, None], inverse[:, None], *[parts[s] for s in starts])
    return smoothed.transpose(1, 0, 2)


def solution(mesh):
    return jax.shard_map(
        local,
        mesh=mesh,
        in_specs=(
            P(None, "cells", None),
            P("cells", "species"),
            P("species"),
            P("species", None),
            P("cells", None),
        ),
        out_specs=P("species", "cells", None),
        check_vma=False,
    )
```
